128 devices in a mesh: gx: 16 (over x, y), gy: 8 (over z, core).
Axes of the slice: x: 4, y: 4, z: 4, core: 2. Of those that a mesh axis runs over, the one named last changes fastest.
Arguments:
- dynamics: float32 [3, 72, 8192], P(None, None, ('gx', 'gy')), may hold values from -6 to 6
- crm_state: float32 [4, 58, 64, 8192], P(None, None, None, ('gx', 'gy')), may hold values from -6 to 6
- density: float32 [58], replicated, may hold values from 0.3 to 1.5
- orientation: int32 [8192], P(('gx', 'gy')), may hold values from 0 to 1
- owner: int32 [8192], P(('gx', 'gy')), may hold values from 0 to 15, as said below
- active: int32 [8192], P(('gx', 'gy')), may hold values from 14 to 58
Outputs:
- dynamics_next: float32 [3, 72, 8192], P(None, None, ('gx', 'gy'))
- crm_next: float32 [4, 58, 64, 16384], P(None, None, None, ('gx', 'gy'))
The draws below stay inside these ranges and needn't reach their ends.
Inputs may be any that keep to these rules, and one draw needn't show every extreme that they name: Among one device's columns at most 8 have any one owner; for every gy index some owner receives exactly 8 columns from every device with that gy index. `orientation`: 0 for the first horizontal direction, 1 for the second.
All inputs are finite; a program needn't handle non-finite values.
Results may differ from the reference program's by a relative error of at most 0.0003.
Values sent between devices are 32-bit elements; how exact they have to be, the bound alone decides.
No kernel may reach another device: no remote copies, remote signals or barrier semaphores. Data moves between devices by JAX's collectives and lax.ppermute only.
A program may use at most 128 MiB of HBM per device.

```python
import math
import jax
import jax.numpy as jnp
from jax import lax

L = 72
NZC = 58
NXC = 64
NSTEP = 2
ITERS = 8
TX = 8
TY = 8
NCOLS = 8192
N_GX = 16
N_GY = 8


def draw_owner(key, part):
    key = jax.random.fold_in(key, 11)
    cols = TX * TY
    cap = 2 * cols // N_GX
    pool = jnp.repeat(jnp.arange(N_GX, dtype=jnp.int32), cap)
    offset = jax.random.randint(jax.random.fold_in(key, 1), (), 0, N_GX)

    def one_tile(tile):
        sub = jax.random.fold_in(key, tile + 2)
        loaded = (offset + tile % N_GY) % N_GX
        order_key = (pool != loaded).astype(jnp.int32) * (4 * cols) + jax.random.permutation(jax.random.fold_in(sub, 0), 2 * cols).astype(jnp.int32)
        chosen = pool[jnp.argsort(order_key, stable=True)][:cols]
        return chosen[jax.random.permutation(jax.random.fold_in(sub, 1), cols)]
    return jax.vmap(one_tile)(jnp.arange(N_GX * N_GY, dtype=jnp.int32)).reshape(-1).astype(jnp.int32)


def place_ends(array, rng, smallest, high):
    spot = [jax.random.randint(jax.random.fold_in(rng, axis), (), 0, length) for axis, length in enumerate(array.shape)]
    widest = array.shape.index(max(array.shape))
    next_to = spot[:widest] + [(spot[widest] + 1) % array.shape[widest]] + spot[widest + 1:]
    return array.at[tuple(spot)].set(smallest).at[tuple(next_to)].set(high)


def shard_levels(rng, dims, split, low, largest):
    level = 1.0
    for axis_at, shards_of in split:
        steps = jax.random.uniform(jax.random.fold_in(jax.random.fold_in(rng, 6), axis_at), (shards_of,), jnp.float32, low / len(split), largest / len(split))
        level = level * jnp.repeat(jnp.exp(steps), dims[axis_at] // shards_of).reshape((-1,) + (1,) * (len(dims) - 1 - axis_at))
    return level


def normal_values(key, shape, deviation, limit, pieces=(), kind=jnp.bfloat16):
    loudness = shard_levels(key, shape, pieces, -0.22, 0.18) if pieces else 1.0
    result = jax.random.normal(key, shape, jnp.float32) * deviation * loudness
    return jnp.minimum(jnp.maximum(result, -limit), limit).astype(kind)


def setup_inputs(seed: int = 0) -> dict:
    streams_of = jax.random.split(jax.random.key(seed), 7)
    dynamics = normal_values(streams_of[0], (3, L, NCOLS), 1.0, 6.0, ((2, 128),), jnp.float32)
    crm_state = normal_values(streams_of[1], (4, NZC, NXC, NCOLS), 1.0, 6.0, ((3, 128),), jnp.float32)
    density = jnp.clip(jnp.exp(jax.random.uniform(streams_of[2], (NZC,), jnp.float32, math.log(0.3), math.log(1.5))), 0.3, 1.5)
    orientation = place_ends(jax.random.randint(streams_of[3], (NCOLS,), 0, 2), jax.random.fold_in(streams_of[3], 1), 0, 1).astype(jnp.int32)
    owner = draw_owner(jax.random.fold_in(streams_of[6], 71), 0)
    active = place_ends(jax.random.randint(streams_of[5], (NCOLS,), NZC // 4, NZC + 1), jax.random.fold_in(streams_of[5], 1), NZC // 4, NZC).astype(jnp.int32)
    return dict(dynamics=dynamics, crm_state=crm_state, density=density, orientation=orientation, owner=owner, active=active)


def shift_up(field):
    return jnp.concatenate([field[1:], jnp.zeros_like(field[:1])], axis=0)


def shift_down(field):
    return jnp.concatenate([jnp.zeros_like(field[:1]), field[:-1]], axis=0)


def lap_x(field):
    return jnp.roll(field, 1, axis=1) + jnp.roll(field, -1, axis=1) - 2.0 * field


def cloud_model(state, force_b, force_u, active_f, density):
    nz = state.shape[1]
    levels = jnp.arange(nz, dtype=jnp.float32)[:, None, None]
    mask = (levels < active_f).astype(jnp.float32)
    rho = density[:, None, None]
    rho_up = 0.5 * (rho + shift_up(rho)) * (levels < nz - 1).astype(jnp.float32)
    rho_dn = shift_down(rho_up)
    diag_term = -(2.0 * rho + rho_up + rho_dn + 0.1 * rho)
    u_wind, w_wind, buoy, press = state[0], state[1], state[2], state[3]
    u_start, b_start = u_wind, buoy

    def sweep(step, press):
        applied = rho * lap_x(press) + rho_up * (shift_up(press) - press) - rho_dn * (press - shift_down(press)) - 0.1 * rho * press
        return press + 0.8 * (rhs_now - applied) / diag_term

    for step in range(NSTEP):
        mean_b = jnp.mean(buoy, axis=1, keepdims=True)
        mean_u = jnp.mean(u_wind, axis=1, keepdims=True)
        b_next = buoy + 0.25 * (force_b - mean_b) + 0.2 * lap_x(buoy) - 0.5 * w_wind
        u_next = u_wind + 0.25 * (force_u - mean_u) + 0.2 * lap_x(u_wind)
        w_next = w_wind + buoy
        flux = rho * w_next
        rhs_now = 0.5 * rho * (jnp.roll(u_next, -1, axis=1) - jnp.roll(u_next, 1, axis=1)) + 0.5 * (shift_up(flux) - shift_down(flux))
        press = lax.fori_loop(0, ITERS, sweep, press)
        u_wind = mask * (u_next - 0.5 * (jnp.roll(press, -1, axis=1) - jnp.roll(press, 1, axis=1)))
        w_wind = mask * (w_next - 0.5 * (shift_up(press) - shift_down(press)))
        buoy = mask * b_next
    tend_b = jnp.mean(buoy - b_start, axis=1, keepdims=True) / NSTEP
    tend_u = jnp.mean(u_wind - u_start, axis=1, keepdims=True) / NSTEP
    return jnp.stack([u_wind, w_wind, buoy, press]), jnp.stack([tend_b, tend_u])


def reference(dynamics, crm_state, density, orientation, owner, active):
    cols = TX * TY
    tiles = N_GX * N_GY
    cap = 2 * cols // N_GX
    force_b = dynamics[0, :NZC]
    force_u = jnp.where(orientation[None, :] == 0, dynamics[1, :NZC], dynamics[2, :NZC])
    active_f = active.astype(jnp.float32)

    def one_tile(tile):
        start = (tile * cols).astype(jnp.int32)
        state = lax.dynamic_slice_in_dim(crm_state, start, cols, axis=3)
        fb = lax.dynamic_slice_in_dim(force_b, start, cols, axis=1)[:, None, :]
        fu = lax.dynamic_slice_in_dim(force_u, start, cols, axis=1)[:, None, :]
        act = lax.dynamic_slice_in_dim(active_f, start, cols, axis=0)[None, None, :]
        return cloud_model(state, fb, fu, act, density)

    finals, tends = lax.map(one_tile, jnp.arange(tiles, dtype=jnp.int32))
    finals = jnp.transpose(finals, (1, 2, 3, 0, 4)).reshape(4, NZC, NXC, tiles * cols)
    tends = jnp.transpose(tends[:, :, :, 0, :], (1, 2, 0, 3)).reshape(2, NZC, tiles * cols)

    owner_t = owner.reshape(tiles, cols)
    onehot = (owner_t[:, :, None] == jnp.arange(N_GX, dtype=jnp.int32)[None, None, :]).astype(jnp.int32)
    rank = jnp.sum(jnp.cumsum(onehot, axis=1) * onehot, axis=2) - 1
    tile_ids = jnp.arange(tiles, dtype=jnp.int32)[:, None]
    row_i = tile_ids // N_GY
    row_j = tile_ids % N_GY
    slot = (owner_t * N_GY + row_j) * (2 * cols) + row_i * cap + rank
    crm_next = jnp.zeros((4, NZC, NXC, tiles * 2 * cols), jnp.float32)
    crm_next = crm_next.at[:, :, :, slot.reshape(-1)].set(finals)

    pad = jnp.zeros((L - NZC, tiles * cols), jnp.float32)
    add_b = jnp.concatenate([tends[0], pad], axis=0)
    add_u = jnp.concatenate([tends[1], pad], axis=0)
    first = (orientation[None, :] == 0).astype(jnp.float32)
    adds = jnp.stack([add_b, first * add_u, (1.0 - first) * add_u])
    grid = dynamics.reshape(3, L, N_GX, N_GY, TX, TY).transpose(0, 1, 2, 4, 3, 5).reshape(3, L, N_GX * TX, N_GY * TY)
    laplace = jnp.roll(grid, 1, 2) + jnp.roll(grid, -1, 2) + jnp.roll(grid, 1, 3) + jnp.roll(grid, -1, 3) - 4.0 * grid
    diffused = (grid + 0.2 * laplace).reshape(3, L, N_GX, TX, N_GY, TY).transpose(0, 1, 2, 4, 3, 5).reshape(3, L, tiles * cols)
    return diffused + adds, crm_next
```

```python
import jax
import jax.numpy as jnp
from jax import lax
from jax.experimental import pallas as pl
from jax.experimental.pallas import tpu as pltpu
from jax.sharding import PartitionSpec as P

NSTEP = 2
ITERS = 8
GROUPS = 16
RANKS = 8
LANES = 128
HALF = 64
QUAD = 4
OCT = 8
MIB = 1024 * 1024


def spans(start, stop, unroll, body):
    turns = (stop - start) // unroll

    def turn(i, carry):
        body([start + i * unroll + k for k in range(unroll)])
        return carry

    if turns:
        lax.fori_loop(0, turns, turn, 0)
    rest = list(range(start + turns * unroll, stop))
    if rest:
        body(rest)


def lane_ids():
    return lax.broadcasted_iota(jnp.int32, (8, LANES), 1)


def to_column(row, rows):
    n = row.shape[1]
    r = lax.broadcasted_iota(jnp.int32, (rows, n), 0)
    c = lax.broadcasted_iota(jnp.int32, (rows, n), 1)
    return jnp.sum(jnp.where(r == c, jnp.broadcast_to(row, (rows, n)), 0.0), axis=1, keepdims=True)


def slot_tables(owner_row, active_row):
    n = owner_row.shape[1]
    own = owner_row.astype(jnp.float32)
    own_col = to_column(own, n)
    r = lax.broadcasted_iota(jnp.int32, (n, n), 0)
    c = lax.broadcasted_iota(jnp.int32, (n, n), 1)
    before = (own_col == jnp.broadcast_to(own, (n, n))) & (c < r)
    rank = jnp.sum(jnp.where(before, 1.0, 0.0), axis=1, keepdims=True)
    slot = own_col * float(RANKS) + rank
    lanes = lax.broadcasted_iota(jnp.int32, (n, LANES), 1).astype(jnp.float32)
    match = jnp.broadcast_to(slot, (n, LANES)) == lanes
    rows = lax.broadcasted_iota(jnp.int32, (n, LANES), 0).astype(jnp.float32)
    act = jnp.broadcast_to(to_column(active_row.astype(jnp.float32), n), (n, LANES))
    column = jnp.sum(jnp.where(match, rows, 0.0), axis=0, keepdims=True)
    active = jnp.sum(jnp.where(match, act, 0.0), axis=0, keepdims=True)
    return jnp.broadcast_to(column, (8, LANES)), jnp.broadcast_to(active, (8, LANES))


def fill_index(idx_ref, column, offset):
    col = column.astype(jnp.int32)
    for m in range(GROUPS):
        turned = pltpu.roll(col, RANKS * m, 1) if m else col
        idx_ref[m] = turned + offset * ((m // QUAD) % 2)


def group_bits():
    group = lane_ids() // RANKS
    return [((group >> b) & 1) == 1 for b in range(4)]


def barrel(rows, bits):
    rows = [rows[-r % GROUPS] for r in range(GROUPS)]
    for b in range(4):
        step = 1 << b
        rows = [jnp.where(bits[b], rows[(r - step) % GROUPS], rows[r]) for r in range(GROUPS)]
    return rows


def take_lanes(value, index):
    return jnp.take_along_axis(value, index, axis=1, mode="promise_in_bounds")


def turn_by(source, target):
    return lax.rem(source - target + GROUPS, GROUPS) * RANKS


def settle(rows):
    return [pltpu.roll(rows[k], LANES - RANKS * k, 1) if k else rows[k] for k in range(GROUPS)]


def mean_x(v):
    while len(v) > 1:
        v = [a + b for a, b in zip(v[::2], v[1::2])]
    total = jnp.sum(v[0], axis=0, keepdims=True)
    return total * (1.0 / 64.0)


def full_width(ref, source):
    cols, levels = source.shape
    ref[...] = jnp.zeros((LANES, LANES), jnp.float32)
    ref[:cols, :levels] = source
    return jnp.transpose(ref[...])


def early_kernel(
    crm, dyn, owner, active, send,
    raw_b, raw_w, dyn_ref, own_ref, act_ref, square, force_ref, vals, picked, stage, idx_ref, sems, small, out_sems,
):
    nz = raw_b.shape[0]
    cols = raw_b.shape[2]
    levels = dyn_ref.shape[2]
    pairs = nz // 2
    cuts = [0, 5, 11, 17, 23, pairs]
    lots = len(cuts) - 1
    few = [
        pltpu.make_async_copy(s, d, small.at[i])
        for i, (s, d) in enumerate(((dyn, dyn_ref), (owner, own_ref), (active, act_ref)))
    ]
    for copy in few:
        copy.start()
    copies = []
    for i in range(lots):
        part = pl.ds(2 * cuts[i], 2 * (cuts[i + 1] - cuts[i]))
        for f, raw in ((2, raw_b), (1, raw_w)):
            copy = pltpu.make_async_copy(crm.at[f, part], raw.at[part], sems.at[i, f - 1])
            copy.start()
            copies.append(copy)
    for copy in few:
        copy.wait()
    me = lax.axis_index("gx")
    column, active_slots = slot_tables(own_ref[...], act_ref[...])
    fill_index(idx_ref, column, 0)
    after = lax.rem(me + 1, GROUPS)
    for owner_at in range(GROUPS):
        stage[owner_at, pairs] = active_slots
        for f in range(3):
            stage[owner_at, pairs + 1 + f, :, :levels] = jnp.where(
                after == owner_at, dyn_ref[f, cols - 8 :, :], dyn_ref[f, :8, :]
            )
    force_ref[...] = full_width(square, dyn_ref[0])
    act = act_ref[...]
    bits = group_bits()

    def level(zs):
        for z in zs:
            force = force_ref[pl.ds(z, 1), :cols]
            mask = jnp.broadcast_to(z < act, (8, cols))
            b = [raw_b[z, pl.ds(m, 8, stride=8), :] for m in range(OCT)]
            w = [raw_w[z, pl.ds(m, 8, stride=8), :] for m in range(OCT)]
            extra = 0.25 * (force - mean_x(b))
            east = b[1:] + [pltpu.roll(b[0], 7, 0)]
            west = [pltpu.roll(b[-1], 1, 0)] + b[:-1]
            b = [
                jnp.where(mask, (0.6 * b[m] + 0.2 * (east[m] + west[m])) + (extra - 0.5 * w[m]), 0.0)
                for m in range(OCT)
            ]
            extra = 0.25 * (force - mean_x(b))
            east = b[1:] + [pltpu.roll(b[0], 7, 0)]
            west = [pltpu.roll(b[-1], 1, 0)] + b[:-1]
            for m in range(OCT):
                vals[z, m, :, :cols] = (1.1 * b[m] + 0.2 * (east[m] + west[m])) + extra

    def pick(gs):
        for m in range(GROUPS):
            for g in gs:
                picked[g, m] = take_lanes(vals[2 * g + m // OCT, m % OCT], idx_ref[m])

    def pack(gs):
        for g in gs:
            rows = barrel([picked[g, m] for m in range(GROUPS)], bits)
            for owner_at in range(GROUPS):
                stage[owner_at, g] = rows[owner_at]

    stores = []
    for i in range(lots):
        copies[2 * i].wait()
        copies[2 * i + 1].wait()
        spans(2 * cuts[i], 2 * cuts[i + 1], 2, level)
        spans(cuts[i], cuts[i + 1], 2, pick)
        spans(cuts[i], cuts[i + 1], 1, pack)
        stop = cuts[i + 1] if i < lots - 1 else stage.shape[1]
        part = pl.ds(cuts[i], stop - cuts[i])
        copy = pltpu.make_async_copy(stage.at[:, part], send.at[:, part], out_sems.at[i])
        copy.start()
        stores.append(copy)
    for copy in stores:
        copy.wait()


def load_raw(ref, z):
    out = []
    for m in range(QUAD):
        low = ref[z, pl.ds(m, 8, stride=8), :]
        high = ref[z, pl.ds(QUAD + m, 8, stride=8), :]
        out.append(jnp.concatenate([low, high], axis=1))
    return out


def east_of(v, low):
    t = pltpu.roll(v[0], HALF, 1)
    return v[1:] + [jnp.where(low, t, pltpu.roll(t, 7, 0))]


def west_of(v, low):
    t = pltpu.roll(v[QUAD - 1], HALF, 1)
    return [jnp.where(low, pltpu.roll(t, 1, 0), t)] + v[:-1]


def packed_mean(v):
    half = mean_x(v)
    return half + pltpu.roll(half, HALF, 1)


def smooth(v, low):
    return [0.6 * a + 0.2 * (b + c) for a, b, c in zip(v, east_of(v, low), west_of(v, low))]


def twice(value):
    return jnp.where(
        lax.broadcasted_iota(jnp.int32, value.shape, 1) < HALF, value, pltpu.roll(value, HALF, 1)
    )


def sweeps(p_ref, rhs_ref, coef_ref, low):
    nz = p_ref.shape[0]
    zero = [jnp.zeros((8, LANES), jnp.float32)] * QUAD

    def one(step, carry):
        below = zero
        here = [p_ref[0, m] for m in range(QUAD)]
        for z in range(nz):
            above = [p_ref[z + 1, m] for m in range(QUAD)] if z < nz - 1 else zero
            kr, ku, kd = (coef_ref[c, pl.ds(z, 1), :] for c in range(3))
            e, w = east_of(here, low), west_of(here, low)
            for m in range(QUAD):
                new = (0.2 * here[m] + rhs_ref[z, m]) + kr * (e[m] + w[m])
                if z < nz - 1:
                    new = new + ku * above[m]
                if z > 0:
                    new = new + kd * below[m]
                p_ref[z, m] = new
            below, here = here, above
        return carry

    lax.fori_loop(0, ITERS, one, 0)


def fill_coefficients(coef_ref, density_row):
    nz = density_row.shape[1]
    rho = jnp.broadcast_to(to_column(density_row, HALF), (HALF, LANES))
    level = lax.broadcasted_iota(jnp.int32, (HALF, LANES), 0)
    above = pltpu.roll(rho, HALF - 1, 0)
    below = pltpu.roll(rho, 1, 0)
    rho_up = jnp.where(level < nz - 1, 0.5 * (rho + above), 0.0)
    rho_dn = jnp.where(level > 0, pltpu.roll(rho_up, 1, 0), 0.0)
    scale = jnp.where(level < nz, 0.8 / (2.1 * rho + rho_up + rho_dn), 0.0)
    coef_ref[0] = scale * rho
    coef_ref[1] = scale * rho_up
    coef_ref[2] = scale * rho_dn
    coef_ref[3] = -0.5 * scale * rho
    coef_ref[4] = -0.5 * scale * above
    coef_ref[5] = 0.5 * scale * below


def main_kernel(
    crm, dyn_ref, orient_ref, owner_ref, active_ref, density_ref,
    send, tend_ref,
    raw, u_ref, w_ref, b_ref, p_ref, rhs_ref, coef_ref, idx_ref, square, force_ref, picked, sems,
):
    nz = p_ref.shape[0]
    cols = raw.shape[3]
    pairs = nz // 2
    copies = []
    for f in range(4):
        copy = pltpu.make_async_copy(crm.at[f], raw.at[f], sems.at[f])
        copy.start()
        copies.append(copy)
    me = lax.axis_index("gx")
    column, _ = slot_tables(owner_ref[...], active_ref[...])
    fill_index(idx_ref, column, HALF)
    fill_coefficients(coef_ref, density_ref[...])
    first = jnp.concatenate([orient_ref[...], orient_ref[...]], axis=1) == 0
    force_ref[0] = twice(full_width(square, dyn_ref[0]))
    wind = full_width(square, dyn_ref[1])
    force_ref[1] = twice(jnp.where(first, wind, full_width(square, dyn_ref[2])))
    act = jnp.concatenate([active_ref[...], active_ref[...]], axis=1)
    low = lane_ids() < HALF
    bits = group_bits()
    tend_ref[...] = jnp.zeros(tend_ref.shape, jnp.float32)
    for copy in copies:
        copy.wait()

    def prologue(zs):
        done = []
        for z in zs:
            mask = jnp.broadcast_to(z < act, (8, LANES))
            fb, fu = force_ref[0, pl.ds(z, 1), :], force_ref[1, pl.ds(z, 1), :]
            b, w, u, p = (load_raw(raw.at[f], z) for f in (2, 1, 0, 3))
            mean_b, mean_u = packed_mean(b), packed_mean(u)
            extra_b, extra_u = 0.25 * (fb - mean_b), 0.25 * (fu - mean_u)
            new_b = [jnp.where(mask, s + (extra_b - 0.5 * a), 0.0) for s, a in zip(smooth(b, low), w)]
            new_u = [s + extra_u for s in smooth(u, low)]
            done.append((z, mean_b, mean_u, new_b, new_u, [x + y for x, y in zip(w, b)], p))
        for z, mean_b, mean_u, new_b, new_u, new_w, p in done:
            tend_ref[0, pl.ds(z, 1), :] = mean_b
            tend_ref[1, pl.ds(z, 1), :] = mean_u
            for m in range(QUAD):
                b_ref[z, m] = new_b[m]
                u_ref[z, m] = new_u[m]
                w_ref[z, m] = new_w[m]
                p_ref[z, m] = p[m]

    spans(0, nz, 4, prologue)

    def right_side(zs):
        for z in zs:
            up = jnp.minimum(z + 1, nz - 1)
            dn = jnp.maximum(z - 1, 0)
            here, cu, cd = (coef_ref[c, pl.ds(z, 1), :] for c in (3, 4, 5))
            u = [u_ref[z, m] for m in range(QUAD)]
            e, w = east_of(u, low), west_of(u, low)
            for m in range(QUAD):
                rhs_ref[z, m] = here * (e[m] - w[m]) + (cu * w_ref[up, m] + cd * w_ref[dn, m])

    spans(0, nz, 4, right_side)
    sweeps(p_ref, rhs_ref, coef_ref, low)

    def middle(zs):
        done = []
        for z in zs:
            mask = jnp.broadcast_to(z < act, (8, LANES))
            fb, fu = force_ref[0, pl.ds(z, 1), :], force_ref[1, pl.ds(z, 1), :]
            p = [p_ref[z, m] for m in range(QUAD)]
            e, w = east_of(p, low), west_of(p, low)
            up, dn = jnp.minimum(z + 1, nz - 1), jnp.maximum(z - 1, 0)
            top = jnp.where(z < nz - 1, 0.5, 0.0)
            bottom = jnp.where(z > 0, 0.5, 0.0)
            us = [jnp.where(mask, u_ref[z, m] - 0.5 * (e[m] - w[m]), 0.0) for m in range(QUAD)]
            ws = [
                jnp.where(mask, w_ref[z, m] - (top * p_ref[up, m] - bottom * p_ref[dn, m]), 0.0)
                for m in range(QUAD)
            ]
            bs = [b_ref[z, m] for m in range(QUAD)]
            mean_b, mean_u, mean_w = packed_mean(bs), packed_mean(us), packed_mean(ws)
            extra = 0.25 * (fu - mean_u)
            last_b = mean_b + 0.25 * (fb - mean_b) - 0.5 * mean_w
            row = z < act
            tb = (jnp.where(row, last_b, 0.0) - tend_ref[0, pl.ds(z, 1), :]) * (1.0 / NSTEP)
            tu = (jnp.where(row, mean_u + extra, 0.0) - tend_ref[1, pl.ds(z, 1), :]) * (1.0 / NSTEP)
            done.append((z, tb, tu, [s + extra for s in smooth(us, low)], [x + y for x, y in zip(ws, bs)]))
        for z, tb, tu, new_u, new_w in done:
            tend_ref[0, pl.ds(z, 1), :] = tb
            tend_ref[1, pl.ds(z, 1), :] = tu
            for m in range(QUAD):
                u_ref[z, m] = new_u[m]
                b_ref[z, m] = new_w[m]

    spans(0, nz, 4, middle)
    sweeps(p_ref, rhs_ref, coef_ref, low)

    def project(zs):
        for z in zs:
            mask = jnp.broadcast_to(z < act, (8, LANES))
            p = [p_ref[z, m] for m in range(QUAD)]
            e, w = east_of(p, low), west_of(p, low)
            for m in range(QUAD):
                w_ref[z, m] = jnp.where(mask, u_ref[z, m] - 0.5 * (e[m] - w[m]), 0.0)

    spans(0, nz, 4, project)
    for f, source in enumerate((p_ref, b_ref, w_ref)):

        def pick(gs):
            for m in range(GROUPS):
                for g in gs:
                    picked[g, m] = take_lanes(source[2 * g + m // OCT, m % QUAD], idx_ref[m])

        def pack(gs):
            for g in gs:
                rows = barrel([picked[g, m] for m in range(GROUPS)], bits)
                for owner_at in range(GROUPS):
                    send[owner_at, f * pairs + g] = pltpu.roll(rows[owner_at], turn_by(me, owner_at), 1)

        spans(0, pairs, 2, pick)
        spans(0, pairs, 2, pack)


def between_kernel(got, dyn_ref, prev_y, next_y, tend_ref, orient_ref, dyn_out, b_out, act_ref, picked):
    pairs = b_out.shape[0] // 2
    cols, levels = dyn_ref.shape[1:]
    me = lax.axis_index("gx")
    bits = group_bits()
    group = lane_ids() // RANKS
    act = jnp.zeros((8, LANES), jnp.float32)
    for source in range(GROUPS):
        act = jnp.where(group == source, pltpu.roll(got[source, pairs], turn_by(source, me), 1), act)
    act_ref[...] = act

    def turn(gs):
        for g in gs:
            for source in range(GROUPS):
                picked[g, source] = pltpu.roll(got[source, g], turn_by(source, me), 1)

    def place(gs):
        for g in gs:
            rows = settle(barrel([picked[g, source] for source in range(GROUPS)], bits))
            for k in range(GROUPS):
                b_out[2 * g + k // OCT, k % OCT] = rows[k]

    spans(0, pairs, 2, turn)
    spans(0, pairs, 2, place)

    left, right = lax.rem(me + GROUPS - 1, GROUPS), lax.rem(me + 1, GROUPS)
    col = lax.broadcasted_iota(jnp.int32, (cols, levels), 0)
    first_b, last_b = col % 8 == 0, col % 8 == 7
    first = jnp.broadcast_to(to_column(orient_ref[...].astype(jnp.float32), cols), (cols, levels)) < 0.5
    adds = [jnp.transpose(tend_ref[i])[:cols, :levels] for i in range(2)]
    adds = [adds[0], jnp.where(first, adds[1], 0.0), jnp.where(first, 0.0, adds[1])]

    def turned(value, by):
        by = by % cols
        return jnp.concatenate([value[cols - by :], value[: cols - by]], axis=0)

    for f in range(3):
        here = dyn_ref[f]
        up_x = jnp.concatenate([got[left, pairs + 1 + f][:, :levels], here[: cols - 8]], axis=0)
        dn_x = jnp.concatenate([here[8:], got[right, pairs + 1 + f][:, :levels]], axis=0)
        up_y = jnp.where(first_b, turned(prev_y[f], -7), turned(here, 1))
        dn_y = jnp.where(last_b, turned(next_y[f], 7), turned(here, -1))
        dyn_out[f] = (here + 0.2 * ((up_x + dn_x) + (up_y + dn_y) - 4.0 * here)) + adds[f]


def last_kernel(got, b_ref, act_ref, out, pressure, stage, out_sems):
    nz = stage.shape[1]
    pairs = nz // 2
    cuts = [0, 6, 12, 18, 24, pairs]
    ahead = [0, 8, 14, 20, 26, pairs]
    lots = len(cuts) - 1
    bits = group_bits()
    act = act_ref[...]
    full = act > 0.0
    for m in range(OCT):
        pressure[0, m] = jnp.zeros((8, LANES), jnp.float32)
        pressure[nz + 1, m] = jnp.zeros((8, LANES), jnp.float32)

    def unpack(f, g):
        return settle(barrel([got[source, f * pairs + g] for source in range(GROUPS)], bits))

    def take_p(gs):
        for g in gs:
            rows = unpack(0, g)
            for k in range(GROUPS):
                z, m = 2 * g + k // OCT, k % OCT
                value = jnp.where(full, rows[k], 0.0)
                pressure[z + 1, m] = value
                stage[3, z, pl.ds(m, 8, stride=8), :] = value

    def take_rest(gs):
        for g in gs:
            w, u = unpack(1, g), unpack(2, g)
            for k in range(GROUPS):
                z, m = 2 * g + k // OCT, k % OCT
                level = z if isinstance(z, int) else z.astype(jnp.float32)
                mask = level < act
                row = pl.ds(m, 8, stride=8)
                gradient = pressure[z + 2, m] - pressure[z, m]
                stage[0, z, row, :] = jnp.where(full, u[k], 0.0)
                stage[1, z, row, :] = jnp.where(mask, w[k] - 0.5 * gradient, 0.0)
                stage[2, z, row, :] = jnp.where(mask, b_ref[z, m] - 0.5 * w[k], 0.0)

    stores = []
    for i in range(lots):
        spans(ahead[i], ahead[i + 1], 2, take_p)
        spans(cuts[i], cuts[i + 1], 2, take_rest)
        part = pl.ds(2 * cuts[i], 2 * (cuts[i + 1] - cuts[i]))
        for f in range(4):
            copy = pltpu.make_async_copy(stage.at[f, part], out.at[f, part], out_sems.at[i, f])
            copy.start()
            stores.append(copy)
    for copy in stores:
        copy.wait()


def per_device(dynamics, crm_state, density, orientation, owner, active):
    nz, nx, cols = crm_state.shape[1:]
    levels = dynamics.shape[1]
    pairs = nz // 2
    f32 = jnp.float32
    vmem = pl.BlockSpec(memory_space=pltpu.VMEM)
    hbm = pl.BlockSpec(memory_space=pltpu.HBM)
    shape = jax.ShapeDtypeStruct
    dma = pltpu.SemaphoreType.DMA
    square = pltpu.VMEM((LANES, LANES), f32)
    index = pltpu.VMEM((GROUPS, 8, LANES), jnp.int32)
    turned = jnp.swapaxes(dynamics, 1, 2)
    owner_row, active_row, orient_row = owner[None], active[None], orientation[None]
    density_row = density[None]
    state_in = pltpu.with_memory_space_constraint(crm_state, pltpu.HBM)

    def params(mib):
        return pltpu.CompilerParams(vmem_limit_bytes=mib * MIB)

    def neighbour(field, axis, by):
        count = lax.axis_size(axis)
        return lax.ppermute(field, axis, [(i, (i + by) % count) for i in range(count)])

    send_b = pl.pallas_call(
        early_kernel,
        out_shape=pltpu.HBM((GROUPS, pairs + 4, 8, LANES), f32),
        in_specs=[hbm] * 4,
        out_specs=hbm,
        scratch_shapes=[
            pltpu.VMEM((nz, nx, cols), f32),
            pltpu.VMEM((nz, nx, cols), f32),
            pltpu.VMEM((3, cols, levels), f32),
            pltpu.VMEM((1, cols), jnp.int32),
            pltpu.VMEM((1, cols), jnp.int32),
            square,
            square,
            pltpu.VMEM((nz, OCT, 8, LANES), f32),
            pltpu.VMEM((pairs, GROUPS, 8, LANES), f32),
            pltpu.VMEM((GROUPS, pairs + 4, 8, LANES), f32),
            index,
            dma((5, 2)),
            dma((3,)),
            dma((5,)),
        ],
        compiler_params=params(16),
        name="early_buoyancy",
    )(state_in, *(pltpu.with_memory_space_constraint(x, pltpu.HBM) for x in (turned, owner_row, active_row)))
    got_b = lax.all_to_all(send_b, "gx", 0, 0, tiled=True)

    state = pltpu.VMEM((nz, QUAD, 8, LANES), f32)
    send, tends = pl.pallas_call(
        main_kernel,
        out_shape=[shape((GROUPS, 3 * pairs, 8, LANES), f32), shape((2, LANES, LANES), f32)],
        in_specs=[hbm, vmem, vmem, vmem, vmem, vmem],
        out_specs=[vmem, vmem],
        scratch_shapes=[pltpu.VMEM((4, nz, nx, cols), f32)]
        + [state] * 5
        + [
            pltpu.VMEM((6, HALF, LANES), f32),
            index,
            square,
            pltpu.VMEM((2, LANES, LANES), f32),
            pltpu.VMEM((pairs, GROUPS, 8, LANES), f32),
            dma((4,)),
        ],
        compiler_params=params(20),
        cost_estimate=pl.CostEstimate(flops=60_000_000, bytes_accessed=14_000_000, transcendentals=0),
        name="cloud_steps",
    )(state_in, turned, orient_row, owner_row, active_row, density_row)
    prev_y, next_y = neighbour(turned, "gy", 1), neighbour(turned, "gy", -1)
    dynamics_next, placed_b, act = pl.pallas_call(
        between_kernel,
        out_shape=[
            shape(turned.shape, f32),
            shape((nz, OCT, 8, LANES), f32),
            shape((8, LANES), f32),
        ],
        in_specs=[vmem] * 6,
        out_specs=[vmem, vmem, vmem],
        scratch_shapes=[pltpu.VMEM((pairs, GROUPS, 8, LANES), f32)],
        compiler_params=params(16),
        name="dynamics_and_b",
    )(got_b, turned, prev_y, next_y, tends, orient_row)

    send, dynamics_next, placed_b, act = lax.optimization_barrier((send, dynamics_next, placed_b, act))
    got = lax.all_to_all(send, "gx", 0, 0, tiled=True)

    crm_next = pl.pallas_call(
        last_kernel,
        out_shape=pltpu.HBM((4, nz, nx, LANES), f32),
        in_specs=[vmem, vmem, vmem],
        out_specs=hbm,
        scratch_shapes=[
            pltpu.VMEM((nz + 2, OCT, 8, LANES), f32),
            pltpu.VMEM((4, nz, nx, LANES), f32),
            dma((5, 4)),
        ],
        compiler_params=params(12),
        name="place_state",
    )(got, placed_b, act)
    return (jnp.swapaxes(dynamics_next, 1, 2), crm_next)


def solution(mesh):
    in_specs = (
        P(None, None, ("gx", "gy")),
        P(None, None, None, ("gx", "gy")),
        P(),
        P(("gx", "gy")),
        P(("gx", "gy")),
        P(("gx", "gy")),
    )
    out_specs = (P(None, None, ("gx", "gy")), P(None, None, None, ("gx", "gy")))
    return jax.shard_map(
        per_device, mesh=mesh, in_specs=in_specs, out_specs=out_specs, check_vma=False
    )
```

```python
import jax
import jax.numpy as jnp
from jax import lax
from jax.experimental import pallas as pl
from jax.experimental.pallas import tpu as pltpu
from jax.sharding import PartitionSpec as P

NSTEP = 2
ITERS = 8
GROUPS = 16
RANKS = 8
LANES = 128
HALF = 64
QUAD = 4
OCT = 8
TAIL = 88
MIB = 1024 * 1024


def spans(start, stop, unroll, body):
    turns = (stop - start) // unroll

    def turn(i, carry):
        body([start + i * unroll + k for k in range(unroll)])
        return carry

    if turns:
        lax.fori_loop(0, turns, turn, 0)
    rest = list(range(start + turns * unroll, stop))
    if rest:
        body(rest)


def lane_ids():
    return lax.broadcasted_iota(jnp.int32, (8, LANES), 1)


def to_column(row, rows):
    n = row.shape[1]
    r = lax.broadcasted_iota(jnp.int32, (rows, n), 0)
    c = lax.broadcasted_iota(jnp.int32, (rows, n), 1)
    return jnp.sum(jnp.where(r == c, jnp.broadcast_to(row, (rows, n)), 0.0), axis=1, keepdims=True)


def slot_tables(owner_row, active_row):
    n = owner_row.shape[1]
    own = owner_row.astype(jnp.float32)
    own_col = to_column(own, n)
    r = lax.broadcasted_iota(jnp.int32, (n, n), 0)
    c = lax.broadcasted_iota(jnp.int32, (n, n), 1)
    before = (own_col == jnp.broadcast_to(own, (n, n))) & (c < r)
    rank = jnp.sum(jnp.where(before, 1.0, 0.0), axis=1, keepdims=True)
    slot = own_col * float(RANKS) + rank
    lanes = lax.broadcasted_iota(jnp.int32, (n, LANES), 1).astype(jnp.float32)
    match = jnp.broadcast_to(slot, (n, LANES)) == lanes
    act = jnp.broadcast_to(to_column(active_row.astype(jnp.float32), n), (n, LANES))
    active = jnp.sum(jnp.where(match, act, 0.0), axis=0, keepdims=True)
    return jnp.where(match, 1.0, 0.0), jnp.broadcast_to(active, (8, LANES))


def in_three(value):
    high = value.astype(jnp.bfloat16)
    rest = value - high.astype(jnp.float32)
    middle = rest.astype(jnp.bfloat16)
    low = (rest - middle.astype(jnp.float32)).astype(jnp.bfloat16)
    return jnp.concatenate([high, middle, low], axis=1)


def to_slots(value, match_ref):
    return jnp.dot(in_three(value), match_ref[...], preferred_element_type=jnp.float32)


def group_bits():
    group = lane_ids() // RANKS
    return [((group >> b) & 1) == 1 for b in range(4)]


def barrel(rows, bits):
    rows = [rows[-r % GROUPS] for r in range(GROUPS)]
    for b in range(4):
        step = 1 << b
        rows = [jnp.where(bits[b], rows[(r - step) % GROUPS], rows[r]) for r in range(GROUPS)]
    return rows


def peer(j, me):
    return lax.rem(j - me + GROUPS, GROUPS)


def mean_x(v):
    while len(v) > 1:
        v = [a + b for a, b in zip(v[::2], v[1::2])]
    total = jnp.sum(v[0], axis=0, keepdims=True)
    return total * (1.0 / 64.0)


def full_width(ref, source):
    cols, levels = source.shape
    ref[...] = jnp.zeros((LANES, LANES), jnp.float32)
    ref[:cols, :levels] = source
    return jnp.transpose(ref[...])


def edge_rows(fields, lane, levels):
    spare = LANES - levels
    row_a = jnp.where(lane < levels, fields[0], pltpu.roll(fields[1], levels, 1))
    row_b = jnp.where(lane < levels, fields[2], pltpu.roll(fields[1], levels - spare, 1))
    return row_a, row_b


def edge_fields(row_a, row_b, lane, levels):
    spare = LANES - levels
    middle = jnp.where(
        lane < spare, pltpu.roll(row_a, spare, 1), pltpu.roll(row_b, LANES - levels + spare, 1)
    )
    return row_a, middle, row_b


def early_kernel(
    crm, dyn, owner, active, send,
    raw_b, raw_w, dyn_ref, wide_ref, own_ref, act_ref, square, force_ref, vals, placed, stage, idx_ref, sems, small, out_sems,
):
    nz = raw_b.shape[0]
    cols = raw_b.shape[2]
    levels = dyn_ref.shape[2]
    pairs = nz // 2
    turns = [0, 3, 6, 9, 12, (pairs + 1) // 2 + 2]
    cuts = [4 * t for t in turns[:-1]] + [nz]
    lots = len(cuts) - 1
    few = [
        pltpu.make_async_copy(s, d, small.at[i])
        for i, (s, d) in enumerate(((dyn, dyn_ref), (owner, own_ref), (active, act_ref)))
    ]
    for copy in few:
        copy.start()
    copies = []
    for i in range(lots):
        part = pl.ds(cuts[i], cuts[i + 1] - cuts[i])
        copies.append(
            [
                pltpu.make_async_copy(crm.at[f, part], raw.at[part], sems.at[i, f - 1])
                for f, raw in ((2, raw_b), (1, raw_w))
            ]
        )
    for lot in copies[:2]:
        for copy in lot:
            copy.start()
    for copy in few:
        copy.wait()
    me = lax.axis_index("gx")
    match, active_slots = slot_tables(own_ref[...], act_ref[...])
    rows = lax.broadcasted_iota(jnp.int32, match.shape, 0).astype(jnp.float32)
    column = jnp.broadcast_to(jnp.sum(match * rows, axis=0, keepdims=True), (8, LANES)).astype(jnp.int32)
    for m in range(GROUPS):
        idx_ref[m] = pltpu.roll(column, lax.rem(me + m, GROUPS) * RANKS, 1)
    after = lax.rem(me + 1, GROUPS)
    wide_ref[:, :, :levels] = dyn_ref[...]
    lane = lane_ids()
    edges = [edge_rows([wide_ref[f, pl.ds(at, 8), :] for f in range(3)], lane, levels) for at in (0, cols - 8)]
    for owner_at in range(GROUPS):
        row_a, row_b = (jnp.where(after == owner_at, far, near) for near, far in zip(*edges))
        ranks = pltpu.roll(active_slots, (TAIL + LANES - RANKS * owner_at) % LANES, 1)
        stage[owner_at, pairs] = row_a
        stage[owner_at, pairs + 1] = jnp.where(lane < TAIL, row_b, ranks)
    force_ref[...] = full_width(square, dyn_ref[0])
    act = act_ref[...]
    bits = group_bits()

    def level(zs):
        for z in zs:
            force = force_ref[pl.ds(z, 1), :cols]
            mask = jnp.broadcast_to(z < act, (8, cols))
            b = [raw_b[z, pl.ds(m, 8, stride=8), :] for m in range(OCT)]
            w = [raw_w[z, pl.ds(m, 8, stride=8), :] for m in range(OCT)]
            extra = 0.25 * (force - mean_x(b))
            east = b[1:] + [pltpu.roll(b[0], 7, 0)]
            west = [pltpu.roll(b[-1], 1, 0)] + b[:-1]
            b = [
                jnp.where(mask, (0.6 * b[m] + 0.2 * (east[m] + west[m])) + (extra - 0.5 * w[m]), 0.0)
                for m in range(OCT)
            ]
            extra = 0.25 * (force - mean_x(b))
            east = b[1:] + [pltpu.roll(b[0], 7, 0)]
            west = [pltpu.roll(b[-1], 1, 0)] + b[:-1]
            for m in range(OCT):
                vals[z, m, :, :cols] = (1.1 * b[m] + 0.2 * (east[m] + west[m])) + extra

    def step(t, carry):
        for half in range(2):
            first, second, third = (jnp.clip(2 * (t - k) + half, 0, pairs - 1) for k in range(3))
            slots = [
                jnp.take_along_axis(
                    vals[2 * second + m // OCT, m % OCT], idx_ref[m], axis=1, mode="promise_in_bounds"
                )
                for m in range(GROUPS)
            ]
            level([2 * first, 2 * first + 1])
            rows = barrel([placed[third, m] for m in range(GROUPS)], bits)
            for j in range(GROUPS):
                stage[peer(j, me), third] = rows[j]
            for m in range(GROUPS):
                placed[second, m] = slots[m]
        return carry

    stores = []
    for i in range(lots):
        for copy in copies[i]:
            copy.wait()
        for lot in copies[i + 2 : i + 3]:
            for copy in lot:
                copy.start()
        lax.fori_loop(turns[i], turns[i + 1], step, 0)
        start = max(2 * (turns[i] - 2), 0)
        stop = 2 * (turns[i + 1] - 2) if i < lots - 1 else stage.shape[1]
        part = pl.ds(start, stop - start)
        copy = pltpu.make_async_copy(stage.at[:, part], send.at[:, part], out_sems.at[i])
        copy.start()
        stores.append(copy)
    for copy in stores:
        copy.wait()


def load_rows(ref, z):
    return [ref[z, pl.ds(m, 8, stride=8), :] for m in range(OCT)]


def side_by_side(v):
    return [jnp.concatenate([v[m], v[QUAD + m]], axis=1) for m in range(QUAD)]


def smooth_rows(v):
    east = v[1:] + [pltpu.roll(v[0], 7, 0)]
    west = [pltpu.roll(v[-1], 1, 0)] + v[:-1]
    return [0.6 * a + 0.2 * (b + c) for a, b, c in zip(v, east, west)]


def east_of(v, low):
    t = pltpu.roll(v[0], HALF, 1)
    return v[1:] + [jnp.where(low, t, pltpu.roll(t, 7, 0))]


def west_of(v, low):
    t = pltpu.roll(v[QUAD - 1], HALF, 1)
    return [jnp.where(low, pltpu.roll(t, 1, 0), t)] + v[:-1]


def packed_mean(v):
    half = mean_x(v)
    return half + pltpu.roll(half, HALF, 1)


def smooth(v, low):
    return [0.6 * a + 0.2 * (b + c) for a, b, c in zip(v, east_of(v, low), west_of(v, low))]


def twice(value):
    return jnp.where(
        lax.broadcasted_iota(jnp.int32, value.shape, 1) < HALF, value, pltpu.roll(value, HALF, 1)
    )


def sweeps(p_ref, rhs_ref, coef_ref, low, nz):
    zero = [jnp.zeros((8, LANES), jnp.float32)] * QUAD

    def one(step, carry):
        below = zero
        here = [p_ref[0, m] for m in range(QUAD)]
        for z in range(nz):
            above = [p_ref[z + 1, m] for m in range(QUAD)] if z < nz - 1 else zero
            kr, ku, kd = (coef_ref[c, pl.ds(z, 1), :] for c in range(3))
            e, w = east_of(here, low), west_of(here, low)
            for m in range(QUAD):
                new = (0.2 * here[m] + rhs_ref[z, m]) + kr * (e[m] + w[m])
                if z < nz - 1:
                    new = new + ku * above[m]
                if z > 0:
                    new = new + kd * below[m]
                p_ref[z, m] = new
            below, here = here, above
        return carry

    lax.fori_loop(0, ITERS, one, 0)


def fill_coefficients(coef_ref, density_row):
    nz = density_row.shape[1]
    rho = jnp.broadcast_to(to_column(density_row, HALF), (HALF, LANES))
    level = lax.broadcasted_iota(jnp.int32, (HALF, LANES), 0)
    above = pltpu.roll(rho, HALF - 1, 0)
    below = pltpu.roll(rho, 1, 0)
    rho_up = jnp.where(level < nz - 1, 0.5 * (rho + above), 0.0)
    rho_dn = jnp.where(level > 0, pltpu.roll(rho_up, 1, 0), 0.0)
    scale = jnp.where(level < nz, 0.8 / (2.1 * rho + rho_up + rho_dn), 0.0)
    coef_ref[0] = scale * rho
    coef_ref[1] = scale * rho_up
    coef_ref[2] = scale * rho_dn
    coef_ref[3] = -0.5 * scale * rho
    coef_ref[4] = -0.5 * scale * above
    coef_ref[5] = 0.5 * scale * below


def main_kernel(
    crm, dyn_ref, orient_ref, owner_ref, active_ref, density_ref,
    send, tend_ref,
    raw, u_ref, w_ref, b_ref, p_ref, rhs_ref, coef_ref, match_ref, square, force_ref, placed, stage, sems, out_sems,
):
    nz = raw.shape[1]
    cols = raw.shape[3]
    pairs = nz // 2
    cuts = [0, 12, 28, 44, nz]
    copies = []
    for i in range(4):
        part = pl.ds(cuts[i], cuts[i + 1] - cuts[i])
        for f in range(4):
            copy = pltpu.make_async_copy(crm.at[f, part], raw.at[f, part], sems.at[i, f])
            copy.start()
            copies.append(copy)
    me = lax.axis_index("gx")
    match, _ = slot_tables(owner_ref[...], active_ref[...])
    match_ref[...] = jnp.zeros(match_ref.shape, jnp.bfloat16)
    for part in range(3):
        for half in range(2):
            at = part * LANES + half * HALF
            match_ref[at : at + HALF, half * LANES : half * LANES + LANES] = match.astype(jnp.bfloat16)
    shifts = [lax.rem(me + m, GROUPS) * RANKS for m in range(GROUPS)]
    fill_coefficients(coef_ref, density_ref[...])
    first = jnp.concatenate([orient_ref[...], orient_ref[...]], axis=1) == 0
    force_ref[0] = twice(full_width(square, dyn_ref[0]))
    wind = full_width(square, dyn_ref[1])
    force_ref[1] = twice(jnp.where(first, wind, full_width(square, dyn_ref[2])))
    narrow = active_ref[...]
    act = jnp.concatenate([narrow, narrow], axis=1)
    low = lane_ids() < HALF
    bits = group_bits()
    tend_ref[...] = jnp.zeros(tend_ref.shape, jnp.float32)

    def prologue(zs):
        for z in zs:
            mask = jnp.broadcast_to(z < narrow, (8, cols))
            fb, fu = force_ref[0, pl.ds(z, 1), :cols], force_ref[1, pl.ds(z, 1), :cols]
            b, w, u, p = (load_rows(raw.at[f], z) for f in (2, 1, 0, 3))
            mean_b, mean_u = mean_x(b), mean_x(u)
            extra_b, extra_u = 0.25 * (fb - mean_b), 0.25 * (fu - mean_u)
            new_b = [jnp.where(mask, s + (extra_b - 0.5 * a), 0.0) for s, a in zip(smooth_rows(b), w)]
            new_u = [s + extra_u for s in smooth_rows(u)]
            new_w = [x + y for x, y in zip(w, b)]
            tend_ref[0, pl.ds(z, 1), :cols] = mean_b
            tend_ref[1, pl.ds(z, 1), :cols] = mean_u
            for ref, rows in ((b_ref, new_b), (u_ref, new_u), (w_ref, new_w), (p_ref, p)):
                for m, value in enumerate(side_by_side(rows)):
                    ref[z, m] = value

    for i in range(4):
        for copy in copies[4 * i : 4 * i + 4]:
            copy.wait()
        spans(cuts[i], cuts[i + 1], 4, prologue)

    def right_side(zs):
        for z in zs:
            up = jnp.minimum(z + 1, nz - 1)
            dn = jnp.maximum(z - 1, 0)
            here, cu, cd = (coef_ref[c, pl.ds(z, 1), :] for c in (3, 4, 5))
            u = [u_ref[z, m] for m in range(QUAD)]
            e, w = east_of(u, low), west_of(u, low)
            for m in range(QUAD):
                rhs_ref[z, m] = here * (e[m] - w[m]) + (cu * w_ref[up, m] + cd * w_ref[dn, m])

    spans(0, nz, 8, right_side)
    sweeps(p_ref, rhs_ref, coef_ref, low, nz)

    def middle(zs):
        done = []
        for z in zs:
            mask = jnp.broadcast_to(z < act, (8, LANES))
            fb, fu = force_ref[0, pl.ds(z, 1), :], force_ref[1, pl.ds(z, 1), :]
            p = [p_ref[z, m] for m in range(QUAD)]
            e, w = east_of(p, low), west_of(p, low)
            up, dn = jnp.minimum(z + 1, nz - 1), jnp.maximum(z - 1, 0)
            top = jnp.where(z < nz - 1, 0.5, 0.0)
            bottom = jnp.where(z > 0, 0.5, 0.0)
            us = [jnp.where(mask, u_ref[z, m] - 0.5 * (e[m] - w[m]), 0.0) for m in range(QUAD)]
            ws = [
                jnp.where(mask, w_ref[z, m] - (top * p_ref[up, m] - bottom * p_ref[dn, m]), 0.0)
                for m in range(QUAD)
            ]
            bs = [b_ref[z, m] for m in range(QUAD)]
            mean_b, mean_u, mean_w = packed_mean(bs), packed_mean(us), packed_mean(ws)
            extra = 0.25 * (fu - mean_u)
            last_b = mean_b + 0.25 * (fb - mean_b) - 0.5 * mean_w
            row = z < act
            tb = (jnp.where(row, last_b, 0.0)[:, :cols] - tend_ref[0, pl.ds(z, 1), :cols]) * (1.0 / NSTEP)
            tu = (jnp.where(row, mean_u + extra, 0.0)[:, :cols] - tend_ref[1, pl.ds(z, 1), :cols]) * (1.0 / NSTEP)
            done.append((z, tb, tu, [s + extra for s in smooth(us, low)], [x + y for x, y in zip(ws, bs)]))
        for z, tb, tu, new_u, new_w in done:
            tend_ref[0, pl.ds(z, 1), :cols] = tb
            tend_ref[1, pl.ds(z, 1), :cols] = tu
            for m in range(QUAD):
                u_ref[z, m] = new_u[m]
                b_ref[z, m] = new_w[m]

    spans(0, nz, 8, middle)
    sweeps(p_ref, rhs_ref, coef_ref, low, nz)

    def project(zs):
        for z in zs:
            mask = jnp.broadcast_to(z < act, (8, LANES))
            p = [p_ref[z, m] for m in range(QUAD)]
            e, w = east_of(p, low), west_of(p, low)
            for m in range(QUAD):
                w_ref[z, m] = jnp.where(mask, u_ref[z, m] - 0.5 * (e[m] - w[m]), 0.0)

    spans(0, nz, 8, project)
    sources = (p_ref, b_ref, w_ref)

    def step(t, carry):
        at = jnp.minimum(t, (pairs - 1) // 2)
        rows = 4 * QUAD * 8
        slots = to_slots(jnp.concatenate([s[pl.ds(4 * at, 4)].reshape(rows, LANES) for s in sources], axis=0), match_ref)
        for half in range(2):
            done = jnp.clip(2 * (t - 1) + half, 0, pairs - 1)
            for f in range(3):
                out = barrel([pltpu.roll(placed[f, done, m], shifts[m], 1) for m in range(GROUPS)], bits)
                for j in range(GROUPS):
                    stage[peer(j, me), f * pairs + done] = out[j]
        for f in range(3):
            for half in range(2):
                for m in range(GROUPS):
                    row = f * rows + 8 * (QUAD * (2 * half + m // OCT) + m % QUAD)
                    col = LANES * ((m // QUAD) % 2)
                    placed[f, 2 * at + half, m] = slots[row : row + 8, col : col + LANES]
        return carry

    stores = []
    turns = [0, 6, 11, (pairs + 1) // 2 + 1]
    for i in range(3):
        lax.fori_loop(turns[i], turns[i + 1], step, 0)
        start, stop = max(2 * (turns[i] - 1), 0), min(2 * (turns[i + 1] - 1), pairs)
        for f in range(3):
            part = pl.ds(f * pairs + start, stop - start)
            copy = pltpu.make_async_copy(stage.at[:, part], send.at[:, part], out_sems.at[i, f])
            copy.start()
            stores.append(copy)
    for copy in stores:
        copy.wait()


def last_kernel(
    got_b, got, dyn_ref, prev_y, next_y, tend_ref, orient_ref,
    out, dyn_out,
    rolled, pressure, stage, out_sems,
):
    nz = stage.shape[1]
    pairs = nz // 2
    cols, levels = dyn_ref.shape[1:]
    me = lax.axis_index("gx")
    bits = group_bits()
    group = lane_ids() // RANKS
    act = jnp.zeros((8, LANES), jnp.float32)
    for source in range(GROUPS):
        ranks = pltpu.roll(got_b[source, pairs + 1], (RANKS * source + LANES - TAIL) % LANES, 1)
        act = jnp.where(group == source, ranks, act)
    full = act > 0.0
    for m in range(OCT):
        pressure[0, m] = jnp.zeros((8, LANES), jnp.float32)
        pressure[nz + 1, m] = jnp.zeros((8, LANES), jnp.float32)
    shifts = [lax.rem(2 * GROUPS - m - me, GROUPS) * RANKS for m in range(GROUPS)]
    peers = [peer(j, me) for j in range(GROUPS)]

    def place(g, m16):
        z, m = 2 * g + m16 // OCT, m16 % OCT
        mask = z.astype(jnp.float32) < act
        row = pl.ds(m, 8, stride=8)
        w = rolled[0, g, m16]
        gradient = pressure[z + 2, m] - pressure[z, m]
        stage[0, z, row, :] = jnp.where(full, rolled[1, g, m16], 0.0)
        stage[1, z, row, :] = jnp.where(mask, w - 0.5 * gradient, 0.0)
        stage[2, z, row, :] = jnp.where(mask, rolled[2, g, m16] - 0.5 * w, 0.0)
        stage[3, z, row, :] = pressure[z + 1, m]

    def keep(f, g, rows):
        for m16 in range(GROUPS):
            if f == 0:
                pressure[2 * g + m16 // OCT + 1, m16 % OCT] = jnp.where(full, rows[m16], 0.0)
            else:
                rolled[f - 1, g, m16] = rows[m16]

    def step(t, carry):
        last = None
        for half in range(2):
            done = jnp.clip(2 * t + half - 3, 0, pairs - 1)
            g = jnp.minimum(2 * t + half, pairs - 1)
            for f, (ref, at) in enumerate(((got, g), (got, pairs + g), (got, 2 * pairs + g), (got_b, g))):
                rows = barrel([ref[peers[j], at] for j in range(GROUPS)], bits)
                rows = [pltpu.roll(rows[m16], shifts[m16], 1) for m16 in range(GROUPS)]
                if last is not None:
                    keep(*last)
                for m16 in range(4 * f, 4 * f + 4):
                    place(done, m16)
                last = (f, g, rows)
        keep(*last)
        return carry

    stores = []
    turns = [0, 5, 8, 11, 14, (pairs + 4) // 2]
    for i in range(5):
        lax.fori_loop(turns[i], turns[i + 1], step, 0)
        start, stop = max(2 * turns[i] - 3, 0), min(2 * turns[i + 1] - 3, pairs)
        part = pl.ds(2 * start, 2 * (stop - start))
        for f in range(4):
            copy = pltpu.make_async_copy(stage.at[f, part], out.at[f, part], out_sems.at[i, f])
            copy.start()
            stores.append(copy)

    left, right = lax.rem(me + GROUPS - 1, GROUPS), lax.rem(me + 1, GROUPS)
    col = lax.broadcasted_iota(jnp.int32, (cols, levels), 0)
    first_b, last_b = col % 8 == 0, col % 8 == 7
    first = jnp.broadcast_to(to_column(orient_ref[...].astype(jnp.float32), cols), (cols, levels)) < 0.5
    adds = [jnp.transpose(tend_ref[i])[:cols, :levels] for i in range(2)]
    adds = [adds[0], jnp.where(first, adds[1], 0.0), jnp.where(first, 0.0, adds[1])]

    def turned(value, by):
        by = by % cols
        return jnp.concatenate([value[cols - by :], value[: cols - by]], axis=0)

    lane = lane_ids()
    before, after = (
        edge_fields(got_b[at, pairs], got_b[at, pairs + 1], lane, levels) for at in (left, right)
    )
    for f in range(3):
        here = dyn_ref[f]
        up_x = jnp.concatenate([before[f][:, :levels], here[: cols - 8]], axis=0)
        dn_x = jnp.concatenate([here[8:], after[f][:, :levels]], axis=0)
        up_y = jnp.where(first_b, turned(prev_y[f], -7), turned(here, 1))
        dn_y = jnp.where(last_b, turned(next_y[f], 7), turned(here, -1))
        dyn_out[f] = (here + 0.2 * ((up_x + dn_x) + (up_y + dn_y) - 4.0 * here)) + adds[f]
    for copy in stores:
        copy.wait()


def per_device(dynamics, crm_state, density, orientation, owner, active):
    nz, nx, cols = crm_state.shape[1:]
    levels = dynamics.shape[1]
    pairs = nz // 2
    f32 = jnp.float32
    vmem = pl.BlockSpec(memory_space=pltpu.VMEM)
    hbm = pl.BlockSpec(memory_space=pltpu.HBM)
    shape = jax.ShapeDtypeStruct
    dma = pltpu.SemaphoreType.DMA
    square = pltpu.VMEM((LANES, LANES), f32)
    turned = jnp.swapaxes(dynamics, 1, 2)
    owner_row, active_row, orient_row = owner[None], active[None], orientation[None]
    density_row = density[None]
    state_in = pltpu.with_memory_space_constraint(crm_state, pltpu.HBM)

    def params(mib):
        return pltpu.CompilerParams(vmem_limit_bytes=mib * MIB)

    def neighbour(field, axis, by):
        count = lax.axis_size(axis)
        return lax.ppermute(field, axis, [(i, (i + by) % count) for i in range(count)])

    send_b = pl.pallas_call(
        early_kernel,
        out_shape=pltpu.HBM((GROUPS, pairs + 2, 8, LANES), f32),
        in_specs=[hbm] * 4,
        out_specs=hbm,
        scratch_shapes=[
            pltpu.VMEM((nz, nx, cols), f32),
            pltpu.VMEM((nz, nx, cols), f32),
            pltpu.VMEM((3, cols, levels), f32),
            pltpu.VMEM((3, cols, LANES), f32),
            pltpu.VMEM((1, cols), jnp.int32),
            pltpu.VMEM((1, cols), jnp.int32),
            square,
            square,
            pltpu.VMEM((nz + 2, OCT, 8, LANES), f32),
            pltpu.VMEM((pairs + 1, GROUPS, 8, LANES), f32),
            pltpu.VMEM((GROUPS, pairs + 2, 8, LANES), f32),
            pltpu.VMEM((GROUPS, 8, LANES), jnp.int32),
            dma((5, 2)),
            dma((3,)),
            dma((5,)),
        ],
        compiler_params=params(16),
        name="early_buoyancy",
    )(state_in, *(pltpu.with_memory_space_constraint(x, pltpu.HBM) for x in (turned, owner_row, active_row)))
    got_b = lax.all_to_all(send_b, "gx", 0, 0, tiled=True)

    state = pltpu.VMEM((nz + 2, QUAD, 8, LANES), f32)
    send, tends = pl.pallas_call(
        main_kernel,
        out_shape=[pltpu.HBM((GROUPS, 3 * pairs, 8, LANES), f32), shape((2, LANES, LANES), f32)],
        in_specs=[hbm, vmem, vmem, vmem, vmem, vmem],
        out_specs=[hbm, vmem],
        scratch_shapes=[pltpu.VMEM((4, nz, nx, cols), f32)]
        + [state] * 5
        + [
            pltpu.VMEM((6, HALF, LANES), f32),
            pltpu.VMEM((3 * LANES, 2 * LANES), jnp.bfloat16),
            square,
            pltpu.VMEM((2, LANES, LANES), f32),
            pltpu.VMEM((3, pairs + 1, GROUPS, 8, LANES), f32),
            pltpu.VMEM((GROUPS, 3 * pairs, 8, LANES), f32),
            dma((4, 4)),
            dma((3, 3)),
        ],
        compiler_params=params(28),
        cost_estimate=pl.CostEstimate(flops=60_000_000, bytes_accessed=14_000_000, transcendentals=0),
        name="cloud_steps",
    )(state_in, turned, orient_row, owner_row, active_row, density_row)
    prev_y, next_y = neighbour(turned, "gy", 1), neighbour(turned, "gy", -1)
    got_b, send, tends, prev_y, next_y = lax.optimization_barrier((got_b, send, tends, prev_y, next_y))
    got = lax.all_to_all(send, "gx", 0, 0, tiled=True)

    crm_next, dynamics_next = pl.pallas_call(
        last_kernel,
        out_shape=[pltpu.HBM((4, nz, nx, LANES), f32), shape(turned.shape, f32)],
        in_specs=[vmem] * 7,
        out_specs=[hbm, vmem],
        scratch_shapes=[
            pltpu.VMEM((3, pairs, GROUPS, 8, LANES), f32),
            pltpu.VMEM((nz + 2, OCT, 8, LANES), f32),
            pltpu.VMEM((4, nz, nx, LANES), f32),
            dma((5, 4)),
        ],
        compiler_params=params(20),
        name="place_state",
    )(got_b, got, turned, prev_y, next_y, tends, orient_row)
    return (jnp.swapaxes(dynamics_next, 1, 2), crm_next)


def solution(mesh):
    in_specs = (
        P(None, None, ("gx", "gy")),
        P(None, None, None, ("gx", "gy")),
        P(),
        P(("gx", "gy")),
        P(("gx", "gy")),
        P(("gx", "gy")),
    )
    out_specs = (P(None, None, ("gx", "gy")), P(None, None, None, ("gx", "gy")))
    return jax.shard_map(
        per_device, mesh=mesh, in_specs=in_specs, out_specs=out_specs, check_vma=False
    )
```

```python
import jax
import jax.numpy as jnp
from jax import lax
from jax.experimental import pallas as pl
from jax.experimental.pallas import tpu as pltpu
from jax.sharding import PartitionSpec as P

NSTEP = 2
ITERS = 8
GROUPS = 16
RANKS = 8
LANES = 128
HALF = 64
QUAD = 4
OCT = 8
TAIL = 88
MIB = 1024 * 1024


def spans(start, stop, unroll, body):
    turns = (stop - start) // unroll

    def turn(i, carry):
        body([start + i * unroll + k for k in range(unroll)])
        return carry

    if turns:
        lax.fori_loop(0, turns, turn, 0)
    rest = list(range(start + turns * unroll, stop))
    if rest:
        body(rest)


def lane_ids():
    return lax.broadcasted_iota(jnp.int32, (8, LANES), 1)


def to_column(row, rows):
    n = row.shape[1]
    r = lax.broadcasted_iota(jnp.int32, (rows, n), 0)
    c = lax.broadcasted_iota(jnp.int32, (rows, n), 1)
    return jnp.sum(jnp.where(r == c, jnp.broadcast_to(row, (rows, n)), 0.0), axis=1, keepdims=True)


def slot_tables(owner_row, active_row):
    n = owner_row.shape[1]
    own = owner_row.astype(jnp.float32)
    own_col = to_column(own, n)
    r = lax.broadcasted_iota(jnp.int32, (n, n), 0)
    c = lax.broadcasted_iota(jnp.int32, (n, n), 1)
    before = (own_col == jnp.broadcast_to(own, (n, n))) & (c < r)
    rank = jnp.sum(jnp.where(before, 1.0, 0.0), axis=1, keepdims=True)
    slot = own_col * float(RANKS) + rank
    lanes = lax.broadcasted_iota(jnp.int32, (n, LANES), 1).astype(jnp.float32)
    match = jnp.broadcast_to(slot, (n, LANES)) == lanes
    act = jnp.broadcast_to(to_column(active_row.astype(jnp.float32), n), (n, LANES))
    active = jnp.sum(jnp.where(match, act, 0.0), axis=0, keepdims=True)
    return jnp.where(match, 1.0, 0.0), jnp.broadcast_to(active, (8, LANES))


def in_three(value):
    high = value.astype(jnp.bfloat16)
    rest = value - high.astype(jnp.float32)
    middle = rest.astype(jnp.bfloat16)
    low = (rest - middle.astype(jnp.float32)).astype(jnp.bfloat16)
    return jnp.concatenate([high, middle, low], axis=1)


def to_slots(value, match_ref):
    return jnp.dot(in_three(value), match_ref[...], preferred_element_type=jnp.float32)


def group_bits():
    group = lane_ids() // RANKS
    return [((group >> b) & 1) == 1 for b in range(4)]


def barrel(rows, bits):
    rows = [rows[-r % GROUPS] for r in range(GROUPS)]
    for b in range(4):
        step = 1 << b
        rows = [jnp.where(bits[b], rows[(r - step) % GROUPS], rows[r]) for r in range(GROUPS)]
    return rows


def peer(j, me):
    return lax.rem(j - me + GROUPS, GROUPS)


def mean_x(v):
    while len(v) > 1:
        v = [a + b for a, b in zip(v[::2], v[1::2])]
    total = jnp.sum(v[0], axis=0, keepdims=True)
    return total * (1.0 / 64.0)


def full_width(ref, source):
    cols, levels = source.shape
    ref[...] = jnp.zeros((LANES, LANES), jnp.float32)
    ref[:cols, :levels] = source
    return jnp.transpose(ref[...])


def edge_rows(fields, lane, levels):
    spare = LANES - levels
    row_a = jnp.where(lane < levels, fields[0], pltpu.roll(fields[1], levels, 1))
    row_b = jnp.where(lane < levels, fields[2], pltpu.roll(fields[1], levels - spare, 1))
    return row_a, row_b


def edge_fields(row_a, row_b, lane, levels):
    spare = LANES - levels
    middle = jnp.where(
        lane < spare, pltpu.roll(row_a, spare, 1), pltpu.roll(row_b, LANES - levels + spare, 1)
    )
    return row_a, middle, row_b


def early_kernel(
    crm, dyn, owner, active, send,
    raw_b, raw_w, dyn_ref, wide_ref, own_ref, act_ref, square, force_ref, vals, placed, stage, idx_ref, sems, small, out_sems,
):
    nz = raw_b.shape[0]
    cols = raw_b.shape[2]
    levels = dyn_ref.shape[2]
    pairs = nz // 2
    turns = [0, 3, 6, 9, 12, (pairs + 1) // 2 + 2]
    cuts = [4 * t for t in turns[:-1]] + [nz]
    lots = len(cuts) - 1
    few = [
        pltpu.make_async_copy(s, d, small.at[i])
        for i, (s, d) in enumerate(((dyn, dyn_ref), (owner, own_ref), (active, act_ref)))
    ]
    for copy in few:
        copy.start()
    copies = []
    for i in range(lots):
        part = pl.ds(cuts[i], cuts[i + 1] - cuts[i])
        copies.append(
            [
                pltpu.make_async_copy(crm.at[f, part], raw.at[part], sems.at[i, f - 1])
                for f, raw in ((2, raw_b), (1, raw_w))
            ]
        )
    for lot in copies[:2]:
        for copy in lot:
            copy.start()
    for copy in few:
        copy.wait()
    me = lax.axis_index("gx")
    match, active_slots = slot_tables(own_ref[...], act_ref[...])
    rows = lax.broadcasted_iota(jnp.int32, match.shape, 0).astype(jnp.float32)
    column = jnp.broadcast_to(jnp.sum(match * rows, axis=0, keepdims=True), (8, LANES)).astype(jnp.int32)
    for m in range(GROUPS):
        idx_ref[m] = pltpu.roll(column, lax.rem(me + m, GROUPS) * RANKS, 1)
    after = lax.rem(me + 1, GROUPS)
    wide_ref[:, :, :levels] = dyn_ref[...]
    lane = lane_ids()
    edges = [edge_rows([wide_ref[f, pl.ds(at, 8), :] for f in range(3)], lane, levels) for at in (0, cols - 8)]
    for owner_at in range(GROUPS):
        row_a, row_b = (jnp.where(after == owner_at, far, near) for near, far in zip(*edges))
        ranks = pltpu.roll(active_slots, (TAIL + LANES - RANKS * owner_at) % LANES, 1)
        stage[owner_at, pairs] = row_a
        stage[owner_at, pairs + 1] = jnp.where(lane < TAIL, row_b, ranks)
    force_ref[...] = full_width(square, dyn_ref[0])
    act = act_ref[...]
    bits = group_bits()

    def level(zs):
        for z in zs:
            force = force_ref[pl.ds(z, 1), :cols]
            mask = jnp.broadcast_to(z < act, (8, cols))
            b = [raw_b[z, pl.ds(m, 8, stride=8), :] for m in range(OCT)]
            w = [raw_w[z, pl.ds(m, 8, stride=8), :] for m in range(OCT)]
            extra = 0.25 * (force - mean_x(b))
            east = b[1:] + [pltpu.roll(b[0], 7, 0)]
            west = [pltpu.roll(b[-1], 1, 0)] + b[:-1]
            b = [
                jnp.where(mask, (0.6 * b[m] + 0.2 * (east[m] + west[m])) + (extra - 0.5 * w[m]), 0.0)
                for m in range(OCT)
            ]
            extra = 0.25 * (force - mean_x(b))
            east = b[1:] + [pltpu.roll(b[0], 7, 0)]
            west = [pltpu.roll(b[-1], 1, 0)] + b[:-1]
            for m in range(OCT):
                vals[z, m, :, :cols] = (1.1 * b[m] + 0.2 * (east[m] + west[m])) + extra

    def step(t, carry):
        for half in range(2):
            first, second, third = (jnp.clip(2 * (t - k) + half, 0, pairs - 1) for k in range(3))
            slots = [
                jnp.take_along_axis(
                    vals[2 * second + m // OCT, m % OCT], idx_ref[m], axis=1, mode="promise_in_bounds"
                )
                for m in range(GROUPS)
            ]
            level([2 * first, 2 * first + 1])
            rows = barrel([placed[third, m] for m in range(GROUPS)], bits)
            for j in range(GROUPS):
                stage[peer(j, me), third] = rows[j]
            for m in range(GROUPS):
                placed[second, m] = slots[m]
        return carry

    stores = []
    for i in range(lots):
        for copy in copies[i]:
            copy.wait()
        for lot in copies[i + 2 : i + 3]:
            for copy in lot:
                copy.start()
        lax.fori_loop(turns[i], turns[i + 1], step, 0)
        start = max(2 * (turns[i] - 2), 0)
        stop = 2 * (turns[i + 1] - 2) if i < lots - 1 else stage.shape[1]
        part = pl.ds(start, stop - start)
        copy = pltpu.make_async_copy(stage.at[:, part], send.at[:, part], out_sems.at[i])
        copy.start()
        stores.append(copy)
    for copy in stores:
        copy.wait()


def load_rows(ref, z):
    return [ref[z, pl.ds(m, 8, stride=8), :] for m in range(OCT)]


def side_by_side(v):
    return [jnp.concatenate([v[m], v[QUAD + m]], axis=1) for m in range(QUAD)]


def smooth_rows(v):
    east = v[1:] + [pltpu.roll(v[0], 7, 0)]
    west = [pltpu.roll(v[-1], 1, 0)] + v[:-1]
    return [0.6 * a + 0.2 * (b + c) for a, b, c in zip(v, east, west)]


def east_of(v, low):
    t = pltpu.roll(v[0], HALF, 1)
    return v[1:] + [jnp.where(low, t, pltpu.roll(t, 7, 0))]


def west_of(v, low):
    t = pltpu.roll(v[QUAD - 1], HALF, 1)
    return [jnp.where(low, pltpu.roll(t, 1, 0), t)] + v[:-1]


def packed_mean(v):
    half = mean_x(v)
    return half + pltpu.roll(half, HALF, 1)


def smooth(v, low):
    return [0.6 * a + 0.2 * (b + c) for a, b, c in zip(v, east_of(v, low), west_of(v, low))]


def twice(value):
    return jnp.where(
        lax.broadcasted_iota(jnp.int32, value.shape, 1) < HALF, value, pltpu.roll(value, HALF, 1)
    )


def sweeps(p_ref, rhs_ref, coef_ref, low, nz):
    zero = [jnp.zeros((8, LANES), jnp.float32)] * QUAD

    def one(step, carry):
        below = zero
        here = [p_ref[0, m] for m in range(QUAD)]
        for z in range(nz):
            above = [p_ref[z + 1, m] for m in range(QUAD)] if z < nz - 1 else zero
            kr, ku, kd = (coef_ref[c, pl.ds(z, 1), :] for c in range(3))
            e, w = east_of(here, low), west_of(here, low)
            for m in range(QUAD):
                new = (0.2 * here[m] + rhs_ref[z, m]) + kr * (e[m] + w[m])
                if z < nz - 1:
                    new = new + ku * above[m]
                if z > 0:
                    new = new + kd * below[m]
                p_ref[z, m] = new
            below, here = here, above
        return carry

    lax.fori_loop(0, ITERS, one, 0)


def fill_coefficients(coef_ref, density_row):
    nz = density_row.shape[1]
    rho = jnp.broadcast_to(to_column(density_row, HALF), (HALF, LANES))
    level = lax.broadcasted_iota(jnp.int32, (HALF, LANES), 0)
    above = pltpu.roll(rho, HALF - 1, 0)
    below = pltpu.roll(rho, 1, 0)
    rho_up = jnp.where(level < nz - 1, 0.5 * (rho + above), 0.0)
    rho_dn = jnp.where(level > 0, pltpu.roll(rho_up, 1, 0), 0.0)
    scale = jnp.where(level < nz, 0.8 / (2.1 * rho + rho_up + rho_dn), 0.0)
    coef_ref[0] = scale * rho
    coef_ref[1] = scale * rho_up
    coef_ref[2] = scale * rho_dn
    coef_ref[3] = -0.5 * scale * rho
    coef_ref[4] = -0.5 * scale * above
    coef_ref[5] = 0.5 * scale * below


def main_kernel(
    crm, dyn_ref, orient_ref, owner_ref, active_ref, density_ref,
    send, tend_ref,
    raw, u_ref, w_ref, b_ref, p_ref, rhs_ref, coef_ref, match_ref, square, force_ref, placed, stage, sems, out_sems,
):
    nz = raw.shape[1]
    cols = raw.shape[3]
    pairs = nz // 2
    cuts = [0, 12, 28, 44, nz]
    copies = []
    for i in range(4):
        part = pl.ds(cuts[i], cuts[i + 1] - cuts[i])
        for f in range(4):
            copy = pltpu.make_async_copy(crm.at[f, part], raw.at[f, part], sems.at[i, f])
            copy.start()
            copies.append(copy)
    me = lax.axis_index("gx")
    match, _ = slot_tables(owner_ref[...], active_ref[...])
    match_ref[...] = jnp.zeros(match_ref.shape, jnp.bfloat16)
    for part in range(3):
        for half in range(2):
            at = part * LANES + half * HALF
            match_ref[at : at + HALF, half * LANES : half * LANES + LANES] = match.astype(jnp.bfloat16)
    shifts = [lax.rem(me + m, GROUPS) * RANKS for m in range(GROUPS)]
    fill_coefficients(coef_ref, density_ref[...])
    first = jnp.concatenate([orient_ref[...], orient_ref[...]], axis=1) == 0
    force_ref[0] = twice(full_width(square, dyn_ref[0]))
    wind = full_width(square, dyn_ref[1])
    force_ref[1] = twice(jnp.where(first, wind, full_width(square, dyn_ref[2])))
    narrow = active_ref[...]
    act = jnp.concatenate([narrow, narrow], axis=1)
    low = lane_ids() < HALF
    bits = group_bits()
    tend_ref[...] = jnp.zeros(tend_ref.shape, jnp.float32)

    def prologue(zs):
        for z in zs:
            mask = jnp.broadcast_to(z < narrow, (8, cols))
            fb, fu = force_ref[0, pl.ds(z, 1), :cols], force_ref[1, pl.ds(z, 1), :cols]
            b, w, u, p = (load_rows(raw.at[f], z) for f in (2, 1, 0, 3))
            mean_b, mean_u = mean_x(b), mean_x(u)
            extra_b, extra_u = 0.25 * (fb - mean_b), 0.25 * (fu - mean_u)
            new_b = [jnp.where(mask, s + (extra_b - 0.5 * a), 0.0) for s, a in zip(smooth_rows(b), w)]
            new_u = [s + extra_u for s in smooth_rows(u)]
            new_w = [x + y for x, y in zip(w, b)]
            tend_ref[0, pl.ds(z, 1), :cols] = mean_b
            tend_ref[1, pl.ds(z, 1), :cols] = mean_u
            for ref, rows in ((b_ref, new_b), (u_ref, new_u), (w_ref, new_w), (p_ref, p)):
                for m, value in enumerate(side_by_side(rows)):
                    ref[z, m] = value

    for i in range(4):
        for copy in copies[4 * i : 4 * i + 4]:
            copy.wait()
        spans(cuts[i], cuts[i + 1], 4, prologue)

    def right_side(zs):
        for z in zs:
            up = jnp.minimum(z + 1, nz - 1)
            dn = jnp.maximum(z - 1, 0)
            here, cu, cd = (coef_ref[c, pl.ds(z, 1), :] for c in (3, 4, 5))
            u = [u_ref[z, m] for m in range(QUAD)]
            e, w = east_of(u, low), west_of(u, low)
            for m in range(QUAD):
                rhs_ref[z, m] = here * (e[m] - w[m]) + (cu * w_ref[up, m] + cd * w_ref[dn, m])

    spans(0, nz, 8, right_side)
    sweeps(p_ref, rhs_ref, coef_ref, low, nz)

    def middle(zs):
        done = []
        for z in zs:
            mask = jnp.broadcast_to(z < act, (8, LANES))
            fb, fu = force_ref[0, pl.ds(z, 1), :], force_ref[1, pl.ds(z, 1), :]
            p = [p_ref[z, m] for m in range(QUAD)]
            e, w = east_of(p, low), west_of(p, low)
            up, dn = jnp.minimum(z + 1, nz - 1), jnp.maximum(z - 1, 0)
            top = jnp.where(z < nz - 1, 0.5, 0.0)
            bottom = jnp.where(z > 0, 0.5, 0.0)
            us = [jnp.where(mask, u_ref[z, m] - 0.5 * (e[m] - w[m]), 0.0) for m in range(QUAD)]
            ws = [
                jnp.where(mask, w_ref[z, m] - (top * p_ref[up, m] - bottom * p_ref[dn, m]), 0.0)
                for m in range(QUAD)
            ]
            bs = [b_ref[z, m] for m in range(QUAD)]
            mean_b, mean_u, mean_w = packed_mean(bs), packed_mean(us), packed_mean(ws)
            extra = 0.25 * (fu - mean_u)
            last_b = mean_b + 0.25 * (fb - mean_b) - 0.5 * mean_w
            row = z < act
            tb = (jnp.where(row, last_b, 0.0)[:, :cols] - tend_ref[0, pl.ds(z, 1), :cols]) * (1.0 / NSTEP)
            tu = (jnp.where(row, mean_u + extra, 0.0)[:, :cols] - tend_ref[1, pl.ds(z, 1), :cols]) * (1.0 / NSTEP)
            done.append((z, tb, tu, [s + extra for s in smooth(us, low)], [x + y for x, y in zip(ws, bs)]))
        for z, tb, tu, new_u, new_w in done:
            tend_ref[0, pl.ds(z, 1), :cols] = tb
            tend_ref[1, pl.ds(z, 1), :cols] = tu
            for m in range(QUAD):
                u_ref[z, m] = new_u[m]
                b_ref[z, m] = new_w[m]

    spans(0, nz, 8, middle)
    sweeps(p_ref, rhs_ref, coef_ref, low, nz)

    def project(zs):
        for z in zs:
            mask = jnp.broadcast_to(z < act, (8, LANES))
            p = [p_ref[z, m] for m in range(QUAD)]
            e, w = east_of(p, low), west_of(p, low)
            for m in range(QUAD):
                w_ref[z, m] = jnp.where(mask, u_ref[z, m] - 0.5 * (e[m] - w[m]), 0.0)

    spans(0, nz, 8, project)
    sources = (p_ref, b_ref, w_ref)

    def step(t, carry):
        at = jnp.minimum(t, (pairs - 1) // 2)
        rows = 4 * QUAD * 8
        slots = to_slots(jnp.concatenate([s[pl.ds(4 * at, 4)].reshape(rows, LANES) for s in sources], axis=0), match_ref)
        for half in range(2):
            done = jnp.clip(2 * (t - 1) + half, 0, pairs - 1)
            for f in range(3):
                out = barrel([pltpu.roll(placed[f, done, m], shifts[m], 1) for m in range(GROUPS)], bits)
                for j in range(GROUPS):
                    stage[peer(j, me), f * pairs + done] = out[j]
        for f in range(3):
            for half in range(2):
                for m in range(GROUPS):
                    row = f * rows + 8 * (QUAD * (2 * half + m // OCT) + m % QUAD)
                    col = LANES * ((m // QUAD) % 2)
                    placed[f, 2 * at + half, m] = slots[row : row + 8, col : col + LANES]
        return carry

    stores = []
    turns = [0, 6, 11, (pairs + 1) // 2 + 1]
    for i in range(3):
        lax.fori_loop(turns[i], turns[i + 1], step, 0)
        start, stop = max(2 * (turns[i] - 1), 0), min(2 * (turns[i + 1] - 1), pairs)
        for f in range(3):
            part = pl.ds(f * pairs + start, stop - start)
            copy = pltpu.make_async_copy(stage.at[:, part], send.at[:, part], out_sems.at[i, f])
            copy.start()
            stores.append(copy)
    for copy in stores:
        copy.wait()


def last_kernel(
    got_b, got, dyn_ref, prev_y, next_y, tend_ref, orient_ref,
    out, dyn_out,
    rolled, pressure, stage, out_sems,
):
    nz = stage.shape[1]
    pairs = nz // 2
    cols, levels = dyn_ref.shape[1:]
    me = lax.axis_index("gx")
    bits = group_bits()
    group = lane_ids() // RANKS
    act = jnp.zeros((8, LANES), jnp.float32)
    for source in range(GROUPS):
        ranks = pltpu.roll(got_b[source, pairs + 1], (RANKS * source + LANES - TAIL) % LANES, 1)
        act = jnp.where(group == source, ranks, act)
    full = act > 0.0
    for m in range(OCT):
        pressure[0, m] = jnp.zeros((8, LANES), jnp.float32)
        pressure[nz + 1, m] = jnp.zeros((8, LANES), jnp.float32)
    shifts = [lax.rem(2 * GROUPS - m - me, GROUPS) * RANKS for m in range(GROUPS)]
    peers = [peer(j, me) for j in range(GROUPS)]

    def place(g, m16):
        z, m = 2 * g + m16 // OCT, m16 % OCT
        mask = z.astype(jnp.float32) < act
        row = pl.ds(m, 8, stride=8)
        w = rolled[0, g, m16]
        gradient = pressure[z + 2, m] - pressure[z, m]
        stage[1, z, row, :] = jnp.where(mask, w - 0.5 * gradient, 0.0)
        stage[2, z, row, :] = jnp.where(mask, rolled[1, g, m16] - 0.5 * w, 0.0)

    def keep(f, g, rows):
        for m16 in range(GROUPS):
            z, m = 2 * g + m16 // OCT, m16 % OCT
            row = pl.ds(m, 8, stride=8)
            if f == 0:
                value = jnp.where(full, rows[m16], 0.0)
                pressure[z + 1, m] = value
                stage[3, z, row, :] = value
            elif f == 2:
                stage[0, z, row, :] = jnp.where(full, rows[m16], 0.0)
            else:
                rolled[f // 2, g, m16] = rows[m16]

    def step(t, carry):
        last = None
        for half in range(2):
            done = jnp.clip(2 * t + half - 3, 0, pairs - 1)
            g = jnp.minimum(2 * t + half, pairs - 1)
            for f, (ref, at) in enumerate(((got, g), (got, pairs + g), (got, 2 * pairs + g), (got_b, g))):
                rows = barrel([ref[peers[j], at] for j in range(GROUPS)], bits)
                rows = [pltpu.roll(rows[m16], shifts[m16], 1) for m16 in range(GROUPS)]
                if last is not None:
                    keep(*last)
                for m16 in range(4 * f, 4 * f + 4):
                    place(done, m16)
                last = (f, g, rows)
        keep(*last)
        return carry

    stores = []
    turns = [0, 5, 8, 11, 14, (pairs + 4) // 2]
    for i in range(5):
        lax.fori_loop(turns[i], turns[i + 1], step, 0)
        start, stop = max(2 * turns[i] - 3, 0), min(2 * turns[i + 1] - 3, pairs)
        part = pl.ds(2 * start, 2 * (stop - start))
        for f in range(4):
            copy = pltpu.make_async_copy(stage.at[f, part], out.at[f, part], out_sems.at[i, f])
            copy.start()
            stores.append(copy)

    left, right = lax.rem(me + GROUPS - 1, GROUPS), lax.rem(me + 1, GROUPS)
    col = lax.broadcasted_iota(jnp.int32, (cols, levels), 0)
    first_b, last_b = col % 8 == 0, col % 8 == 7
    first = jnp.broadcast_to(to_column(orient_ref[...].astype(jnp.float32), cols), (cols, levels)) < 0.5
    adds = [jnp.transpose(tend_ref[i])[:cols, :levels] for i in range(2)]
    adds = [adds[0], jnp.where(first, adds[1], 0.0), jnp.where(first, 0.0, adds[1])]

    def turned(value, by):
        by = by % cols
        return jnp.concatenate([value[cols - by :], value[: cols - by]], axis=0)

    lane = lane_ids()
    before, after = (
        edge_fields(got_b[at, pairs], got_b[at, pairs + 1], lane, levels) for at in (left, right)
    )
    for f in range(3):
        here = dyn_ref[f]
        up_x = jnp.concatenate([before[f][:, :levels], here[: cols - 8]], axis=0)
        dn_x = jnp.concatenate([here[8:], after[f][:, :levels]], axis=0)
        up_y = jnp.where(first_b, turned(prev_y[f], -7), turned(here, 1))
        dn_y = jnp.where(last_b, turned(next_y[f], 7), turned(here, -1))
        dyn_out[f] = (here + 0.2 * ((up_x + dn_x) + (up_y + dn_y) - 4.0 * here)) + adds[f]
    for copy in stores:
        copy.wait()


def per_device(dynamics, crm_state, density, orientation, owner, active):
    nz, nx, cols = crm_state.shape[1:]
    levels = dynamics.shape[1]
    pairs = nz // 2
    f32 = jnp.float32
    vmem = pl.BlockSpec(memory_space=pltpu.VMEM)
    hbm = pl.BlockSpec(memory_space=pltpu.HBM)
    shape = jax.ShapeDtypeStruct
    dma = pltpu.SemaphoreType.DMA
    square = pltpu.VMEM((LANES, LANES), f32)
    turned = jnp.swapaxes(dynamics, 1, 2)
    owner_row, active_row, orient_row = owner[None], active[None], orientation[None]
    density_row = density[None]
    state_in = pltpu.with_memory_space_constraint(crm_state, pltpu.HBM)

    def params(mib):
        return pltpu.CompilerParams(vmem_limit_bytes=mib * MIB)

    def neighbour(field, axis, by):
        count = lax.axis_size(axis)
        return lax.ppermute(field, axis, [(i, (i + by) % count) for i in range(count)])

    send_b = pl.pallas_call(
        early_kernel,
        out_shape=pltpu.HBM((GROUPS, pairs + 2, 8, LANES), f32),
        in_specs=[hbm] * 4,
        out_specs=hbm,
        scratch_shapes=[
            pltpu.VMEM((nz, nx, cols), f32),
            pltpu.VMEM((nz, nx, cols), f32),
            pltpu.VMEM((3, cols, levels), f32),
            pltpu.VMEM((3, cols, LANES), f32),
            pltpu.VMEM((1, cols), jnp.int32),
            pltpu.VMEM((1, cols), jnp.int32),
            square,
            square,
            pltpu.VMEM((nz + 2, OCT, 8, LANES), f32),
            pltpu.VMEM((pairs + 1, GROUPS, 8, LANES), f32),
            pltpu.VMEM((GROUPS, pairs + 2, 8, LANES), f32),
            pltpu.VMEM((GROUPS, 8, LANES), jnp.int32),
            dma((5, 2)),
            dma((3,)),
            dma((5,)),
        ],
        compiler_params=params(16),
        name="early_buoyancy",
    )(state_in, *(pltpu.with_memory_space_constraint(x, pltpu.HBM) for x in (turned, owner_row, active_row)))
    got_b = lax.all_to_all(send_b, "gx", 0, 0, tiled=True)

    state = pltpu.VMEM((nz + 2, QUAD, 8, LANES), f32)
    send, tends = pl.pallas_call(
        main_kernel,
        out_shape=[pltpu.HBM((GROUPS, 3 * pairs, 8, LANES), f32), shape((2, LANES, LANES), f32)],
        in_specs=[hbm, vmem, vmem, vmem, vmem, vmem],
        out_specs=[hbm, vmem],
        scratch_shapes=[pltpu.VMEM((4, nz, nx, cols), f32)]
        + [state] * 5
        + [
            pltpu.VMEM((6, HALF, LANES), f32),
            pltpu.VMEM((3 * LANES, 2 * LANES), jnp.bfloat16),
            square,
            pltpu.VMEM((2, LANES, LANES), f32),
            pltpu.VMEM((3, pairs + 1, GROUPS, 8, LANES), f32),
            pltpu.VMEM((GROUPS, 3 * pairs, 8, LANES), f32),
            dma((4, 4)),
            dma((3, 3)),
        ],
        compiler_params=params(28),
        cost_estimate=pl.CostEstimate(flops=60_000_000, bytes_accessed=14_000_000, transcendentals=0),
        name="cloud_steps",
    )(state_in, turned, orient_row, owner_row, active_row, density_row)
    prev_y, next_y = neighbour(turned, "gy", 1), neighbour(turned, "gy", -1)
    got_b, send, tends, prev_y, next_y = lax.optimization_barrier((got_b, send, tends, prev_y, next_y))
    got = lax.all_to_all(send, "gx", 0, 0, tiled=True)

    crm_next, dynamics_next = pl.pallas_call(
        last_kernel,
        out_shape=[pltpu.HBM((4, nz, nx, LANES), f32), shape(turned.shape, f32)],
        in_specs=[vmem] * 7,
        out_specs=[hbm, vmem],
        scratch_shapes=[
            pltpu.VMEM((2, pairs, GROUPS, 8, LANES), f32),
            pltpu.VMEM((nz + 2, OCT, 8, LANES), f32),
            pltpu.VMEM((4, nz, nx, LANES), f32),
            dma((5, 4)),
        ],
        compiler_params=params(20),
        name="place_state",
    )(got_b, got, turned, prev_y, next_y, tends, orient_row)
    return (jnp.swapaxes(dynamics_next, 1, 2), crm_next)


def solution(mesh):
    in_specs = (
        P(None, None, ("gx", "gy")),
        P(None, None, None, ("gx", "gy")),
        P(),
        P(("gx", "gy")),
        P(("gx", "gy")),
        P(("gx", "gy")),
    )
    out_specs = (P(None, None, ("gx", "gy")), P(None, None, None, ("gx", "gy")))
    return jax.shard_map(
        per_device, mesh=mesh, in_specs=in_specs, out_specs=out_specs, check_vma=False
    )
```
